32 devices in a mesh: dp: 8 (over z, core), tensor: 4 (over y, x).
Axes of the slice: x: 2, y: 2, z: 4, core: 2. Of those that a mesh axis runs over, the one named last changes fastest.
Arguments:
- tokens: bfloat16 [16384, 1024], P(('dp', 'tensor')), may hold values from -6 to 6
- gain_one: float32 [1024], replicated, may hold values from 0.25 to 1.75
- in_weight: bfloat16 [1024, 3, 1024], P('dp', None, 'tensor'), may hold values from -0.1875 to 0.1875
- conv_weight: float32 [3, 1024], replicated, may hold values from -3 to 3
- out_weight: bfloat16 [1024, 1024], P('tensor', 'dp'), may hold values from -0.1875 to 0.1875
- gain_two: float32 [1024], replicated, may hold values from 0.25 to 1.75
- gate_weight: bfloat16 [1024, 4608], P('dp', 'tensor'), may hold values from -0.1875 to 0.1875
- up_weight: bfloat16 [1024, 4608], P('dp', 'tensor'), may hold values from -0.1875 to 0.1875
- down_weight: bfloat16 [4608, 1024], P('tensor', 'dp'), may hold values from -0.09375 to 0.09375
- out_cotangent: bfloat16 [16384, 1024], P(('dp', 'tensor')), may hold values from -6 to 6
Outputs:
- block_out: bfloat16 [16384, 1024], P(('dp', 'tensor'))
- token_grad: float32 [16384, 1024], P(('dp', 'tensor'))
- gain_one_grad: float32 [1024], replicated
- in_weight_grad: float32 [1024, 3, 1024], P('dp', None, 'tensor')
- conv_weight_grad: float32 [3, 1024], replicated
- out_weight_grad: float32 [1024, 1024], P('tensor', 'dp')
- gain_two_grad: float32 [1024], replicated
- gate_weight_grad: float32 [1024, 4608], P('dp', 'tensor')
- up_weight_grad: float32 [1024, 4608], P('dp', 'tensor')
- down_weight_grad: float32 [4608, 1024], P('tensor', 'dp')
The draws below stay inside these ranges and needn't reach their ends.
All inputs are finite; a program needn't handle non-finite values.
Results may differ from the reference program's by a relative error of at most 0.017.
Values may be sent and summed in bfloat16 or wider, within the bound.
A program may use at most 192 MiB of HBM per device.

```python
import jax
import jax.numpy as jnp
from jax import lax

D = 1024
FF = 4608
SEQ_LEN = 2048
TOKENS = 16384


def steps_of(key, extent, split, least, top_value):
    gain = 1.0
    for position, parts in split:
        heights = jax.random.uniform(jax.random.fold_in(jax.random.fold_in(key, 6), position), (parts,), jnp.float32, least / len(split), top_value / len(split))
        gain = gain * jnp.repeat(jnp.exp(heights), extent[position] // parts).reshape((-1,) + (1,) * (len(extent) - 1 - position))
    return gain


def normal_values(key, shape, width, bound, shards=(), held_as=jnp.bfloat16):
    entries = width * jax.random.normal(key, shape, jnp.float32)
    if shards:
        entries = entries * steps_of(key, shape, shards, -0.22, 0.18)
    return jnp.clip(entries, -bound, bound).astype(held_as)


def setup_inputs(seed: int = 0) -> dict:
    streams_of = jax.random.split(jax.random.key(seed), 11)
    return {
        "tokens": normal_values(streams_of[0], (TOKENS, D), 1.0, 6.0, ((0, 32),)),
        "gain_one": jnp.clip(1.0 + 0.15 * jax.random.normal(streams_of[1], (D,), jnp.float32), 0.25, 1.75),
        "in_weight": normal_values(streams_of[2], (D, 3, D), D ** -0.5, 0.1875, ((0, 8), (2, 4))),
        "conv_weight": normal_values(streams_of[3], (3, D), 0.6, 3.0, (), jnp.float32),
        "out_weight": normal_values(streams_of[4], (D, D), D ** -0.5, 0.1875, ((0, 4), (1, 8))),
        "gain_two": jnp.clip(1.0 + 0.15 * jax.random.normal(streams_of[5], (D,), jnp.float32), 0.25, 1.75),
        "gate_weight": normal_values(streams_of[6], (D, FF), D ** -0.5, 0.1875, ((0, 8), (1, 4))),
        "up_weight": normal_values(streams_of[7], (D, FF), D ** -0.5, 0.1875, ((0, 8), (1, 4))),
        "down_weight": normal_values(streams_of[8], (FF, D), FF ** -0.5, 0.09375, ((0, 4), (1, 8))),
        "out_cotangent": normal_values(streams_of[9], (TOKENS, D), 1.0, 6.0, ((0, 32),)),
    }


epsilon = 1e-05
highest = lax.Precision.HIGHEST

@jax.custom_vjp
def low(v):
    return lax.optimization_barrier(v.astype(jnp.bfloat16)).astype(jnp.float32)

@jax.custom_vjp
def low_back(v):
    return v

def low_keep(v):
    return (low(v), None)

def low_pass(kept, grad):
    return (grad,)

def back_keep(v):
    return (v, None)

def back_low(kept, grad):
    return (low(grad),)
low.defvjp(low_keep, low_pass)
low_back.defvjp(back_keep, back_low)

def rms_norm(values, norm_gain):
    return values * lax.rsqrt(lax.optimization_barrier(jnp.mean(values * values, axis=-1, keepdims=True)) + epsilon) * norm_gain

def matmul(former, latter):
    return jnp.dot(former, latter, precision=highest)

def block_forward(token_rows, weights):
    gain_one, in_weight, conv_weight, out_weight, gain_two, gate_weight, up_weight, down_weight = weights
    length = token_rows.shape[0]
    model_width = token_rows.shape[1]
    normed_one = low(rms_norm(token_rows, gain_one))
    projected = matmul(normed_one, in_weight.reshape(model_width, 3 * model_width))
    projected = low_back(projected.reshape(length, 3, model_width))
    gate_b = projected[:, 0]
    gate_c = projected[:, 1]
    values_x = projected[:, 2]
    gated_input = gate_b * values_x
    padded = jnp.pad(gated_input, ((2, 0), (0, 0)))
    convolved = conv_weight[0] * gated_input + conv_weight[1] * padded[1:-1] + conv_weight[2] * padded[:-2]
    mixer_out = low(gate_c * convolved)
    residual = token_rows + low_back(matmul(mixer_out, out_weight))
    normed_two = low(rms_norm(residual, gain_two))
    gate_act = low_back(matmul(normed_two, gate_weight))
    up_act = low_back(matmul(normed_two, up_weight))
    hidden = low(jax.nn.silu(gate_act) * up_act)
    return residual + low_back(matmul(hidden, down_weight))

def reference(tokens, gain_one, in_weight, conv_weight, out_weight, gain_two, gate_weight, up_weight, down_weight, out_cotangent):
    params = tuple((weight_item.astype(jnp.float32) for weight_item in (gain_one, in_weight, conv_weight, out_weight, gain_two, gate_weight, up_weight, down_weight)))
    sequences = tokens.astype(jnp.float32).reshape(-1, SEQ_LEN, D)
    cotangents = out_cotangent.astype(jnp.float32).reshape(-1, SEQ_LEN, D)

    def one_sequence(totals, sequence_pair):
        token_rows, cotangent = sequence_pair
        result, pullback = jax.vjp(block_forward, token_rows, params)
        gradients = pullback(cotangent)
        totals = tuple((total_item + grad_item for total_item, grad_item in zip(totals, gradients[1])))
        return (totals, (result.astype(jnp.bfloat16), gradients[0]))
    zeros_init = tuple((jnp.zeros_like(weight_item) for weight_item in params))
    totals, outputs = lax.scan(one_sequence, zeros_init, (sequences, cotangents))
    block_out = outputs[0].reshape(-1, D)
    token_grad = outputs[1].reshape(-1, D)
    return (block_out, token_grad, totals[0], totals[1], totals[2], totals[3], totals[4], totals[5], totals[6], totals[7])
```

```python
import jax
import jax.numpy as jnp
from jax import lax
from jax.sharding import PartitionSpec as P

SEQ_LEN = 2048


epsilon = 1e-05


def matmul(former, latter):
    return jnp.dot(former, latter, preferred_element_type=jnp.float32)


def matmul_nt(former, latter):
    return lax.dot_general(
        former, latter, (((1,), (1,)), ((), ())), preferred_element_type=jnp.float32
    )


def matmul_tn(former, latter):
    return lax.dot_general(
        former, latter, (((0,), (0,)), ((), ())), preferred_element_type=jnp.float32
    )


def rms_forward(values, norm_gain):
    inverse_rms = lax.rsqrt(jnp.mean(values * values, axis=-1, keepdims=True) + epsilon)
    return (values * inverse_rms * norm_gain, inverse_rms)


def rms_backward(values, inverse_rms, norm_gain, incoming):
    weighted = incoming * norm_gain
    normed = values * inverse_rms
    return inverse_rms * (
        weighted - normed * jnp.mean(weighted * normed, axis=-1, keepdims=True)
    )


def ring_pairs(axis):
    length = lax.axis_size(axis)
    return [(i, (i + 1) % length) for i in range(length)]


def ring_gather(block, axis):
    length = lax.axis_size(axis)
    me = lax.axis_index(axis)
    rows = block.shape[0]
    whole = jnp.zeros((length * rows, block.shape[1]), block.dtype)
    whole = lax.dynamic_update_slice(whole, block, (me * rows, 0))
    for step in range(1, length):
        block = lax.ppermute(block, axis, ring_pairs(axis))
        owner = (me - step + length) % length
        whole = lax.dynamic_update_slice(whole, block, (owner * rows, 0))
    return (whole, block)


def ring_scatter(terms, axis):
    length = lax.axis_size(axis)
    me = lax.axis_index(axis)
    rows = terms.shape[0] // length

    def own(step):
        block = (me - 1 - step + 2 * length) % length
        return lax.dynamic_slice(terms, (block * rows, 0), (rows, terms.shape[1]))

    total = own(0)
    for step in range(1, length):
        arrived = lax.ppermute(total.astype(jnp.bfloat16), axis, ring_pairs(axis))
        total = arrived.astype(jnp.float32) + own(step).astype(jnp.float32)
    return total.astype(jnp.float32)


def gather_rows(rows):
    return lax.all_gather(rows, "tensor", axis=0, tiled=True)


def scatter_rows(partial):
    return lax.psum_scatter(
        partial.astype(jnp.bfloat16), "tensor", scatter_dimension=0, tiled=True
    ).astype(jnp.float32)


def lagged(array, by):
    return jnp.pad(array, ((by, 0), (0, 0)))[: array.shape[0]]


def leading(array, by):
    return jnp.pad(array, ((0, by), (0, 0)))[by:]


def local(
    tokens,
    gain_one,
    in_weight,
    conv_weight,
    out_weight,
    gain_two,
    gate_weight,
    up_weight,
    down_weight,
    out_cotangent,
):
    width = tokens.shape[1]
    part = in_weight.shape[0]
    channels = in_weight.shape[2]
    units = gate_weight.shape[1]

    token_rows = tokens.astype(jnp.float32)
    normed_one, inverse_one = rms_forward(token_rows, gain_one)
    normed_all = gather_rows(normed_one.astype(jnp.bfloat16))
    cotangent_all = gather_rows(out_cotangent)

    mixer_part = jnp.concatenate(
        [in_weight.reshape(part, 3 * channels), out_weight.T], axis=1
    )
    mixer_full, last = ring_gather(mixer_part, "dp")
    in_full = mixer_full[:, : 3 * channels]
    out_turned = mixer_full[:, 3 * channels :]
    ffn_part = jnp.concatenate([gate_weight, up_weight, down_weight.T], axis=1)
    ffn_part, last = lax.optimization_barrier((ffn_part, last))
    ffn_full, _ = ring_gather(ffn_part, "dp")
    front_full = ffn_full[:, : 2 * units]
    down_turned = ffn_full[:, 2 * units :]

    channel_start = lax.axis_index("tensor") * channels
    taps = lax.dynamic_slice(conv_weight, (0, channel_start), (3, channels))
    row_count = normed_all.shape[0]
    positions = lax.broadcasted_iota(jnp.int32, (row_count, 1), 0) % SEQ_LEN

    projected = matmul(normed_all, in_full)
    gate_b = projected[:, :channels]
    gate_c = projected[:, channels : 2 * channels]
    values_x = projected[:, 2 * channels :]
    gated_input = gate_b * values_x
    lag_one = jnp.where(positions >= 1, lagged(gated_input, 1), 0.0)
    lag_two = jnp.where(positions >= 2, lagged(gated_input, 2), 0.0)
    convolved = taps[0] * gated_input + taps[1] * lag_one + taps[2] * lag_two
    mixer_low = (gate_c * convolved).astype(jnp.bfloat16)
    residual = token_rows + scatter_rows(matmul_nt(mixer_low, out_turned))

    normed_two, inverse_two = rms_forward(residual, gain_two)
    normed_two_all = gather_rows(normed_two.astype(jnp.bfloat16))

    front = matmul(normed_two_all, front_full)
    gate_act = front[:, :units]
    up_act = front[:, units:]
    grad_hidden = matmul(cotangent_all, down_turned)
    sigmoid_gate = jax.nn.sigmoid(gate_act)
    silu_gate = gate_act * sigmoid_gate
    hidden = (silu_gate * up_act).astype(jnp.bfloat16)
    grad_gate = (
        grad_hidden * up_act * sigmoid_gate * (1.0 + gate_act * (1.0 - sigmoid_gate))
    ).astype(jnp.bfloat16)
    grad_up = (grad_hidden * silu_gate).astype(jnp.bfloat16)
    grad_front = jnp.concatenate([grad_gate, grad_up], axis=1)
    grad_two = scatter_rows(matmul_nt(grad_front, front_full))
    block_out = (residual + scatter_rows(matmul_nt(hidden, down_turned))).astype(jnp.bfloat16)

    down_terms = matmul_tn(cotangent_all, hidden).astype(jnp.bfloat16)
    front_terms = matmul_tn(normed_two_all, grad_front)
    gain_two_grad = (
        jnp.sum(front_terms * front_full.astype(jnp.float32), axis=1) / gain_two
    )
    front_terms = front_terms.astype(jnp.bfloat16)
    down_grad = ring_scatter(down_terms, "dp")
    front_grad = ring_scatter(front_terms, "dp")

    grad_resid = out_cotangent.astype(jnp.float32) + rms_backward(
        residual, inverse_two, gain_two, grad_two
    )
    branch_all = gather_rows(grad_resid.astype(jnp.bfloat16))

    grad_mixer = matmul(branch_all, out_turned)
    out_terms = matmul_tn(branch_all, mixer_low)
    grad_conv = grad_mixer * gate_c
    lead_one = leading(jnp.where(positions >= 1, grad_conv, 0.0), 1)
    lead_two = leading(jnp.where(positions >= 2, grad_conv, 0.0), 2)
    grad_gated = taps[0] * grad_conv + taps[1] * lead_one + taps[2] * lead_two
    grad_proj = jnp.concatenate(
        [
            (grad_gated * values_x).astype(jnp.bfloat16),
            (grad_mixer * convolved).astype(jnp.bfloat16),
            (grad_gated * gate_b).astype(jnp.bfloat16),
        ],
        axis=1,
    )
    grad_one = scatter_rows(matmul_nt(grad_proj, in_full))
    in_terms = matmul_tn(normed_all, grad_proj)
    tap_grad = jnp.stack(
        [
            jnp.sum(grad_conv * gated_input, axis=0),
            jnp.sum(grad_conv * lag_one, axis=0),
            jnp.sum(grad_conv * lag_two, axis=0),
        ]
    )
    gain_one_grad = jnp.sum(in_terms * in_full.astype(jnp.float32), axis=1) / gain_one
    tap_full = lax.dynamic_update_slice(
        jnp.zeros((3, width), jnp.float32), tap_grad, (0, channel_start)
    )
    small = jnp.concatenate([gain_one_grad[None], gain_two_grad[None], tap_full], axis=0)
    small = lax.psum(small, ("dp", "tensor"))

    mixer_terms = jnp.concatenate(
        [in_terms.astype(jnp.bfloat16), out_terms.astype(jnp.bfloat16)], axis=1
    )
    mixer_grad = ring_scatter(mixer_terms, "dp")

    token_grad = grad_resid + rms_backward(token_rows, inverse_one, gain_one, grad_one)
    return (
        block_out,
        token_grad,
        small[0],
        mixer_grad[:, : 3 * channels].reshape(part, 3, channels),
        small[2:],
        mixer_grad[:, 3 * channels :].T,
        small[1],
        front_grad[:, :units],
        front_grad[:, units:],
        down_grad.T,
    )


def solution(mesh):
    return jax.shard_map(
        local,
        mesh=mesh,
        in_specs=(
            P(("dp", "tensor"), None),
            P(),
            P("dp", None, "tensor"),
            P(),
            P("tensor", "dp"),
            P(),
            P("dp", "tensor"),
            P("dp", "tensor"),
            P("tensor", "dp"),
            P(("dp", "tensor"), None),
        ),
        out_specs=(
            P(("dp", "tensor"), None),
            P(("dp", "tensor"), None),
            P(),
            P("dp", None, "tensor"),
            P(),
            P("tensor", "dp"),
            P(),
            P("dp", "tensor"),
            P("dp", "tensor"),
            P("tensor", "dp"),
        ),
        check_vma=False,
    )
```

```python
import jax
import jax.numpy as jnp
from jax import lax
from jax.experimental import pallas as pl
from jax.experimental.pallas import tpu as pltpu
from jax.sharding import PartitionSpec as P

SEQ_LEN = 2048


epsilon = 1e-05


def matmul(former, latter):
    return jnp.dot(former, latter, preferred_element_type=jnp.float32)


def matmul_nt(former, latter):
    return lax.dot_general(
        former, latter, (((1,), (1,)), ((), ())), preferred_element_type=jnp.float32
    )


def matmul_tn(former, latter):
    return lax.dot_general(
        former, latter, (((0,), (0,)), ((), ())), preferred_element_type=jnp.float32
    )


def rms_forward(values, norm_gain):
    inverse_rms = lax.rsqrt(jnp.mean(values * values, axis=-1, keepdims=True) + epsilon)
    return (values * inverse_rms * norm_gain, inverse_rms)


def rms_backward(values, inverse_rms, norm_gain, incoming):
    weighted = incoming * norm_gain
    normed = values * inverse_rms
    return inverse_rms * (
        weighted - normed * jnp.mean(weighted * normed, axis=-1, keepdims=True)
    )


def gather_rows(rows):
    return lax.all_gather(rows, "tensor", axis=0, tiled=True)


def scatter_rows(partial):
    return lax.psum_scatter(
        partial.astype(jnp.bfloat16), "tensor", scatter_dimension=0, tiled=True
    ).astype(jnp.float32)


MESH = pl.DeviceIdType.MESH
CHUNK = 16


def add_rows(target, terms, rows):
    def body(i, carry):
        where = pl.ds(pl.multiple_of(i * CHUNK, CHUNK), CHUNK)
        total = terms[0][where, :].astype(jnp.float32)
        for term in terms[1:]:
            total = total + term[where, :].astype(jnp.float32)
        target[where, :] = total.astype(target.dtype)
        return carry

    lax.fori_loop(0, rows // CHUNK, body, 0)


def exchange(identity, gathers=(), reduces=(), spread=(), fold=(), small=None):
    n = lax.axis_size("dp")
    t = lax.axis_size("tensor")
    square = bool(spread or fold)
    arrays = [*gathers, *reduces, *spread, *fold] + ([small] if small is not None else [])
    anyspace = pl.BlockSpec(memory_space=pl.ANY)
    vmem = pl.BlockSpec(memory_space=pltpu.VMEM)
    in_specs, out_specs, out_shape, scratch = [], [], [], []
    dma = pltpu.SemaphoreType.DMA
    for g in gathers:
        in_specs.append(anyspace)
        out_specs.append(anyspace)
        out_shape.append(jax.ShapeDtypeStruct((n, *g.shape), g.dtype))
        scratch += [dma((n,)), dma((n,)), dma((1,))]
    for r in reduces:
        in_specs.append(vmem)
        out_specs.append(vmem)
        out_shape.append(jax.ShapeDtypeStruct(r.shape[1:], jnp.float32))
        scratch += [dma((n,)), dma((n,)), pltpu.VMEM((n - 1, *r.shape[1:]), r.dtype)]
    for s in spread:
        in_specs.append(anyspace)
        out_specs.append(anyspace)
        out_shape.append(jax.ShapeDtypeStruct((t, *s.shape), s.dtype))
        scratch += [dma((6,)), dma((6,)), dma((1,))]
    for f in fold:
        in_specs.append(vmem)
        out_specs.append(vmem)
        out_shape.append(jax.ShapeDtypeStruct(f.shape[1:], jnp.float32))
        scratch += [dma((6,)), dma((6,)), pltpu.VMEM((6, *f.shape[2:]), f.dtype)]
    if small is not None:
        in_specs.append(vmem)
        out_specs.append(vmem)
        out_shape.append(jax.ShapeDtypeStruct(small.shape, jnp.float32))
        scratch += [
            dma((n + t,)),
            dma((n + t,)),
            pltpu.VMEM((t, *small.shape), jnp.float32),
            pltpu.VMEM((n, *small.shape), jnp.float32),
        ]

    def kernel(*refs):
        ins = refs[: len(arrays)]
        outs = refs[len(arrays) : 2 * len(arrays)]
        rest = list(refs[2 * len(arrays) :])
        parts = []
        for i in range(len(arrays)):
            count = 4 if small is not None and i == len(arrays) - 1 else 3
            parts.append((ins[i], outs[i], *rest[:count]))
            rest = rest[count:]
        ng, nr, ns, nf = len(gathers), len(reduces), len(spread), len(fold)
        p_gather = parts[:ng]
        p_reduce = parts[ng : ng + nr]
        p_spread = parts[ng + nr : ng + nr + ns]
        p_fold = parts[ng + nr + ns : ng + nr + ns + nf]
        p_small = parts[ng + nr + ns + nf :]

        me = lax.axis_index("dp")
        mine = lax.axis_index("tensor")
        right = lax.rem(me + 1, n)
        left = lax.rem(me + n - 1, n)
        xn = mine + 1 - 2 * lax.rem(mine, 2)
        yn = lax.rem(mine + 2, 4)
        opposite = lax.rem(xn + 2, 4)

        barrier = pltpu.get_barrier_semaphore()
        if small is not None:
            greeted = [("dp", lax.rem(me + k, n)) for k in range(1, n)]
            greeted += [("tensor", lax.rem(mine + k, t)) for k in range(1, t)]
        else:
            greeted = [("dp", left), ("dp", right)] if (gathers or reduces) else []
            greeted += [("tensor", xn), ("tensor", yn)] if square else []
        for axis, who in greeted:
            pl.semaphore_signal(barrier, inc=1, device_id={axis: who}, device_id_type=MESH)
        pl.semaphore_wait(barrier, len(greeted))

        sent, kept = [], []

        def send(src, dst, sems, slot, axis, who):
            copy = pltpu.make_async_remote_copy(
                src_ref=src,
                dst_ref=dst,
                send_sem=sems[0].at[slot],
                recv_sem=sems[1].at[slot],
                device_id={axis: who},
                device_id_type=MESH,
            )
            copy.start()
            sent.append(copy)
            return copy

        ring_g = [
            send(x, o.at[me], (a, b), 0, "dp", right) for x, o, a, b, _ in p_gather
        ]
        ring_r = [
            send(x.at[lax.rem(me + n - 1, n)], held.at[0], (a, b), 0, "dp", right)
            for x, o, a, b, held in p_reduce
        ]
        spread_c = []
        for x, o, a, b, _ in p_spread:
            spread_c.append(
                [
                    send(x.at[0], o.at[mine, 0], (a, b), 0, "tensor", xn),
                    send(x.at[1], o.at[mine, 1], (a, b), 1, "tensor", yn),
                    send(x.at[1], o.at[mine, 1], (a, b), 2, "tensor", xn),
                    send(x.at[0], o.at[mine, 0], (a, b), 3, "tensor", yn),
                ]
            )
        fold_c = []
        for x, o, a, b, got in p_fold:
            fold_c.append(
                [
                    send(x.at[opposite, 1], got.at[0], (a, b), 0, "tensor", xn),
                    send(x.at[opposite, 0], got.at[1], (a, b), 1, "tensor", yn),
                    send(x.at[xn, 1], got.at[2], (a, b), 2, "tensor", xn),
                    send(x.at[yn, 0], got.at[3], (a, b), 3, "tensor", yn),
                ]
            )
        for x, o, a, b, near, far in p_small:
            small_c = [
                send(x, near.at[mine], (a, b), k, "tensor", lax.rem(mine + k, t))
                for k in range(1, t)
            ]
        for x, o, a, b, local_sem in p_gather:
            kept.append(pltpu.make_async_copy(x, o.at[me], local_sem.at[0]))
            kept[-1].start()
        for x, o, a, b, local_sem in p_spread:
            kept.append(pltpu.make_async_copy(x, o.at[mine], local_sem.at[0]))
            kept[-1].start()

        def second_phase():
            for (x, o, a, b, _), c in zip(p_spread, spread_c):
                c[0].wait_recv()
                c.append(send(o.at[xn, 0], o.at[xn, 0], (a, b), 4, "tensor", yn))
                c[1].wait_recv()
                c.append(send(o.at[yn, 1], o.at[yn, 1], (a, b), 5, "tensor", xn))
            for (x, o, a, b, got), c in zip(p_fold, fold_c):
                half = x.shape[2]
                c[0].wait_recv()
                add_rows(got.at[0], [got.at[0], x.at[yn, 1]], half)
                c.append(send(got.at[0], got.at[5], (a, b), 5, "tensor", yn))
                c[1].wait_recv()
                add_rows(got.at[1], [got.at[1], x.at[xn, 0]], half)
                c.append(send(got.at[1], got.at[4], (a, b), 4, "tensor", xn))
            for x, o, a, b, near, far in p_small:
                near[mine] = x[...]
                for c in small_c:
                    c.wait_recv()
                total = near[0]
                for k in range(1, t):
                    total = total + near[k]
                far[me] = total
                for k in range(1, n):
                    small_c.append(
                        send(far.at[me], far.at[me], (a, b), t + k, "dp", lax.rem(me + k, n))
                    )

        for step in range(n - 1):
            if step == 2:
                second_phase()
            for i, (x, o, a, b, _) in enumerate(p_gather):
                block = lax.rem(me - step - 1 + n, n)
                ring_g[i].wait_recv()
                if step < n - 2:
                    ring_g[i] = send(o.at[block], o.at[block], (a, b), step + 1, "dp", right)
            for i, (x, o, a, b, held) in enumerate(p_reduce):
                block = lax.rem(me - step - 2 + 2 * n, n)
                ring_r[i].wait_recv()
                rows = x.shape[1]
                if step < n - 2:
                    add_rows(held.at[step], [held.at[step], x.at[block]], rows)
                    ring_r[i] = send(
                        held.at[step], held.at[step + 1], (a, b), step + 1, "dp", right
                    )
                else:
                    add_rows(o, [held.at[step], x.at[block]], rows)

        for c in spread_c:
            for k in (2, 3, 4, 5):
                c[k].wait_recv()
        for (x, o, a, b, got), c in zip(p_fold, fold_c):
            half = x.shape[2]
            for k in (2, 3, 4, 5):
                c[k].wait_recv()
            add_rows(o.at[0], [x.at[mine, 0], got.at[3], got.at[4]], half)
            add_rows(o.at[1], [x.at[mine, 1], got.at[2], got.at[5]], half)
        for x, o, a, b, near, far in p_small:
            for c in small_c[t - 1 :]:
                c.wait_recv()
            total = far[0]
            for k in range(1, n):
                total = total + far[k]
            o[...] = total
        for copy in kept:
            copy.wait()
        for copy in sent:
            copy.wait_send()

    moved = sum(array.size * array.dtype.itemsize for array in arrays)
    return pl.pallas_call(
        kernel,
        out_shape=out_shape,
        in_specs=in_specs,
        out_specs=out_specs,
        scratch_shapes=scratch,
        compiler_params=pltpu.CompilerParams(
            collective_id=identity, has_side_effects=True, vmem_limit_bytes=40 * 2**20
        ),
        cost_estimate=pl.CostEstimate(
            flops=moved, bytes_accessed=40 * moved, transcendentals=0
        ),
    )(*arrays)


def halves(rows):
    return rows.reshape(2, rows.shape[0] // 2, rows.shape[1])


def quarters(partial):
    t = lax.axis_size("tensor")
    return partial.astype(jnp.bfloat16).reshape(
        t, 2, partial.shape[0] // (2 * t), partial.shape[1]
    )


def spread_with(identity, rows, **ring):
    if lax.axis_size("tensor") == 4:
        *others, whole = exchange(identity, spread=[halves(rows)], **ring)
        return (whole.reshape(-1, rows.shape[1]), *others)
    return (gather_rows(rows), *exchange(identity, **ring))


def fold_with(identity, partial, small=None, **ring):
    if lax.axis_size("tensor") == 4:
        results = list(exchange(identity, fold=[quarters(partial)], small=small, **ring))
        total = results.pop(len(ring.get("gathers", ())) + len(ring.get("reduces", ())))
        return (total.reshape(-1, partial.shape[1]), *results)
    return (scatter_rows(partial), *exchange(identity, small=small, **ring))


def stacked(blocks):
    return blocks.reshape(-1, blocks.shape[2])


def unstacked(terms):
    n = lax.axis_size("dp")
    return terms.astype(jnp.bfloat16).reshape(n, terms.shape[0] // n, terms.shape[1])


def lagged(array, by):
    return jnp.pad(array, ((by, 0), (0, 0)))[: array.shape[0]]


def leading(array, by):
    return jnp.pad(array, ((0, by), (0, 0)))[by:]


def local(
    tokens,
    gain_one,
    in_weight,
    conv_weight,
    out_weight,
    gain_two,
    gate_weight,
    up_weight,
    down_weight,
    out_cotangent,
):
    width = tokens.shape[1]
    part = in_weight.shape[0]
    channels = in_weight.shape[2]
    units = gate_weight.shape[1]

    token_rows = tokens.astype(jnp.float32)
    normed_one, inverse_one = rms_forward(token_rows, gain_one)

    mixer_part = jnp.concatenate(
        [in_weight.reshape(part, 3 * channels), out_weight.T], axis=1
    )
    normed_all, mixer_blocks = spread_with(
        1, normed_one.astype(jnp.bfloat16), gathers=[mixer_part]
    )
    mixer_full = stacked(mixer_blocks)
    in_full = mixer_full[:, : 3 * channels]
    out_turned = mixer_full[:, 3 * channels :]
    cotangent_rows, normed_all = lax.optimization_barrier((out_cotangent, normed_all))
    cotangent_all = gather_rows(cotangent_rows)
    front_part = jnp.concatenate([gate_weight, up_weight], axis=1)

    channel_start = lax.axis_index("tensor") * channels
    taps = lax.dynamic_slice(conv_weight, (0, channel_start), (3, channels))
    row_count = normed_all.shape[0]
    positions = lax.broadcasted_iota(jnp.int32, (row_count, 1), 0) % SEQ_LEN

    projected = matmul(normed_all, in_full)
    gate_b = projected[:, :channels]
    gate_c = projected[:, channels : 2 * channels]
    values_x = projected[:, 2 * channels :]
    gated_input = gate_b * values_x
    lag_one = jnp.where(positions >= 1, lagged(gated_input, 1), 0.0)
    lag_two = jnp.where(positions >= 2, lagged(gated_input, 2), 0.0)
    convolved = taps[0] * gated_input + taps[1] * lag_one + taps[2] * lag_two
    mixer_low = (gate_c * convolved).astype(jnp.bfloat16)
    mixer_sum, front_blocks = fold_with(
        2, matmul_nt(mixer_low, out_turned), gathers=[front_part]
    )
    front_full = stacked(front_blocks)
    residual = token_rows + mixer_sum

    normed_two, inverse_two = rms_forward(residual, gain_two)
    normed_two_all, down_blocks = spread_with(
        3, normed_two.astype(jnp.bfloat16), gathers=[down_weight.T]
    )
    down_turned = stacked(down_blocks)

    front = matmul(normed_two_all, front_full)
    gate_act = front[:, :units]
    up_act = front[:, units:]
    grad_hidden = matmul(cotangent_all, down_turned)
    sigmoid_gate = jax.nn.sigmoid(gate_act)
    silu_gate = gate_act * sigmoid_gate
    hidden = (silu_gate * up_act).astype(jnp.bfloat16)
    grad_gate = (
        grad_hidden * up_act * sigmoid_gate * (1.0 + gate_act * (1.0 - sigmoid_gate))
    ).astype(jnp.bfloat16)
    grad_up = (grad_hidden * silu_gate).astype(jnp.bfloat16)
    grad_front = jnp.concatenate([grad_gate, grad_up], axis=1)
    block_out = (residual + scatter_rows(matmul_nt(hidden, down_turned))).astype(jnp.bfloat16)

    down_terms = matmul_tn(cotangent_all, hidden)
    grad_two, down_grad = fold_with(
        4, matmul_nt(grad_front, front_full), reduces=[unstacked(down_terms)]
    )
    front_terms = matmul_tn(normed_two_all, grad_front)
    gain_two_grad = (
        jnp.sum(front_terms * front_full.astype(jnp.float32), axis=1) / gain_two
    )

    grad_resid = out_cotangent.astype(jnp.float32) + rms_backward(
        residual, inverse_two, gain_two, grad_two
    )
    branch_all, front_grad = spread_with(
        5, grad_resid.astype(jnp.bfloat16), reduces=[unstacked(front_terms)]
    )

    grad_mixer = matmul(branch_all, out_turned)
    out_terms = matmul_tn(branch_all, mixer_low)
    grad_conv = grad_mixer * gate_c
    lead_one = leading(jnp.where(positions >= 1, grad_conv, 0.0), 1)
    lead_two = leading(jnp.where(positions >= 2, grad_conv, 0.0), 2)
    grad_gated = taps[0] * grad_conv + taps[1] * lead_one + taps[2] * lead_two
    grad_proj = jnp.concatenate(
        [
            (grad_gated * values_x).astype(jnp.bfloat16),
            (grad_mixer * convolved).astype(jnp.bfloat16),
            (grad_gated * gate_b).astype(jnp.bfloat16),
        ],
        axis=1,
    )
    in_terms = matmul_tn(normed_all, grad_proj)
    tap_grad = jnp.stack(
        [
            jnp.sum(grad_conv * gated_input, axis=0),
            jnp.sum(grad_conv * lag_one, axis=0),
            jnp.sum(grad_conv * lag_two, axis=0),
        ]
    )
    gain_one_grad = jnp.sum(in_terms * in_full.astype(jnp.float32), axis=1) / gain_one
    tap_full = lax.dynamic_update_slice(
        jnp.zeros((3, width), jnp.float32), tap_grad, (0, channel_start)
    )
    small = jnp.concatenate(
        [gain_one_grad[None], gain_two_grad[None], tap_full, jnp.zeros_like(tap_full)], axis=0
    )
    mixer_terms = jnp.concatenate(
        [in_terms.astype(jnp.bfloat16), out_terms.astype(jnp.bfloat16)], axis=1
    )
    grad_one, mixer_grad, small = fold_with(
        6, matmul_nt(grad_proj, in_full), small=small, reduces=[unstacked(mixer_terms)]
    )

    token_grad = grad_resid + rms_backward(token_rows, inverse_one, gain_one, grad_one)
    return (
        block_out,
        token_grad,
        small[0],
        mixer_grad[:, : 3 * channels].reshape(part, 3, channels),
        small[2:5],
        mixer_grad[:, 3 * channels :].T,
        small[1],
        front_grad[:, :units],
        front_grad[:, units:],
        down_grad.T,
    )


def solution(mesh):
    return jax.shard_map(
        local,
        mesh=mesh,
        in_specs=(
            P(("dp", "tensor"), None),
            P(),
            P("dp", None, "tensor"),
            P(),
            P("tensor", "dp"),
            P(),
            P("dp", "tensor"),
            P("dp", "tensor"),
            P("tensor", "dp"),
            P(("dp", "tensor"), None),
        ),
        out_specs=(
            P(("dp", "tensor"), None),
            P(("dp", "tensor"), None),
            P(),
            P("dp", None, "tensor"),
            P(),
            P("tensor", "dp"),
            P(),
            P("dp", "tensor"),
            P("dp", "tensor"),
            P("tensor", "dp"),
        ),
        check_vma=False,
    )
```

```python
import jax
import jax.numpy as jnp
from jax import lax
from jax.experimental import pallas as pl
from jax.experimental.pallas import tpu as pltpu
from jax.sharding import PartitionSpec as P

SEQ_LEN = 2048


epsilon = 1e-05


def matmul(former, latter):
    return jnp.dot(former, latter, preferred_element_type=jnp.float32)


def matmul_nt(former, latter):
    return lax.dot_general(
        former, latter, (((1,), (1,)), ((), ())), preferred_element_type=jnp.float32
    )


def matmul_tn(former, latter):
    return lax.dot_general(
        former, latter, (((0,), (0,)), ((), ())), preferred_element_type=jnp.float32
    )


def rms_forward(values, norm_gain):
    inverse_rms = lax.rsqrt(jnp.mean(values * values, axis=-1, keepdims=True) + epsilon)
    return (values * inverse_rms * norm_gain, inverse_rms)


def rms_backward(values, inverse_rms, norm_gain, incoming):
    weighted = incoming * norm_gain
    normed = values * inverse_rms
    return inverse_rms * (
        weighted - normed * jnp.mean(weighted * normed, axis=-1, keepdims=True)
    )


def gather_rows(rows):
    return lax.all_gather(rows, "tensor", axis=0, tiled=True)


def scatter_rows(partial):
    return lax.psum_scatter(
        partial.astype(jnp.bfloat16), "tensor", scatter_dimension=0, tiled=True
    ).astype(jnp.float32)


MESH = pl.DeviceIdType.MESH
CHUNK = 16


def add_rows(target, terms, rows):
    def body(i, carry):
        where = pl.ds(pl.multiple_of(i * CHUNK, CHUNK), CHUNK)
        total = terms[0][where, :].astype(jnp.float32)
        for term in terms[1:]:
            total = total + term[where, :].astype(jnp.float32)
        target[where, :] = total.astype(target.dtype)
        return carry

    lax.fori_loop(0, rows // CHUNK, body, 0)


def exchange(identity, gathers=(), reduces=(), spread=(), fold=(), small=None):
    n = lax.axis_size("dp")
    t = lax.axis_size("tensor")
    square = bool(spread or fold)
    ahead = n // 2
    back = n - 1 - ahead
    step_bytes = sum(g.size * g.dtype.itemsize for g in gathers)
    step_bytes += sum(r.size * r.dtype.itemsize for r in reduces) // n
    middle = ahead - 1 if step_bytes < 400_000 else min(2, ahead - 1)
    arrays = [*gathers, *reduces, *spread, *fold] + ([small] if small is not None else [])
    anyspace = pl.BlockSpec(memory_space=pl.ANY)
    vmem = pl.BlockSpec(memory_space=pltpu.VMEM)
    in_specs, out_specs, out_shape, scratch = [], [], [], []
    dma = pltpu.SemaphoreType.DMA
    for g in gathers:
        in_specs.append(anyspace)
        out_specs.append(anyspace)
        out_shape.append(jax.ShapeDtypeStruct((n, *g.shape), g.dtype))
        scratch += [dma((n,)), dma((n,)), dma((1,))]
    for r in reduces:
        in_specs.append(vmem)
        out_specs.append(vmem)
        out_shape.append(jax.ShapeDtypeStruct(r.shape[1:], jnp.float32))
        scratch += [dma((n,)), dma((n,)), pltpu.VMEM((n - 1, *r.shape[1:]), r.dtype)]
    for s in spread:
        in_specs.append(anyspace)
        out_specs.append(anyspace)
        out_shape.append(jax.ShapeDtypeStruct((t, *s.shape), s.dtype))
        scratch += [dma((6,)), dma((6,)), dma((1,))]
    for f in fold:
        in_specs.append(vmem)
        out_specs.append(vmem)
        out_shape.append(jax.ShapeDtypeStruct(f.shape[1:], jnp.float32))
        scratch += [dma((6,)), dma((6,)), pltpu.VMEM((6, *f.shape[2:]), f.dtype)]
    if small is not None:
        in_specs.append(vmem)
        out_specs.append(vmem)
        out_shape.append(jax.ShapeDtypeStruct(small.shape, jnp.float32))
        scratch += [
            dma((n + t,)),
            dma((n + t,)),
            pltpu.VMEM((t, *small.shape), jnp.float32),
            pltpu.VMEM((n, *small.shape), jnp.float32),
        ]

    def kernel(*refs):
        ins = refs[: len(arrays)]
        outs = refs[len(arrays) : 2 * len(arrays)]
        rest = list(refs[2 * len(arrays) :])
        parts = []
        for i in range(len(arrays)):
            count = 4 if small is not None and i == len(arrays) - 1 else 3
            parts.append((ins[i], outs[i], *rest[:count]))
            rest = rest[count:]
        ng, nr, ns, nf = len(gathers), len(reduces), len(spread), len(fold)
        p_gather = parts[:ng]
        p_reduce = parts[ng : ng + nr]
        p_spread = parts[ng + nr : ng + nr + ns]
        p_fold = parts[ng + nr + ns : ng + nr + ns + nf]
        p_small = parts[ng + nr + ns + nf :]

        me = lax.axis_index("dp")
        mine = lax.axis_index("tensor")
        right = lax.rem(me + 1, n)
        left = lax.rem(me + n - 1, n)
        xn = mine + 1 - 2 * lax.rem(mine, 2)
        yn = lax.rem(mine + 2, 4)
        opposite = lax.rem(xn + 2, 4)

        barrier = pltpu.get_barrier_semaphore()
        if small is not None:
            greeted = [("dp", lax.rem(me + k, n)) for k in range(1, n)]
            greeted += [("tensor", lax.rem(mine + k, t)) for k in range(1, t)]
        else:
            greeted = [("dp", left), ("dp", right)] if (gathers or reduces) else []
            greeted += [("tensor", xn), ("tensor", yn)] if square else []
        for axis, who in greeted:
            pl.semaphore_signal(barrier, inc=1, device_id={axis: who}, device_id_type=MESH)
        pl.semaphore_wait(barrier, len(greeted))

        sent, kept = [], []

        def send(src, dst, sems, slot, axis, who):
            copy = pltpu.make_async_remote_copy(
                src_ref=src,
                dst_ref=dst,
                send_sem=sems[0].at[slot],
                recv_sem=sems[1].at[slot],
                device_id={axis: who},
                device_id_type=MESH,
            )
            copy.start()
            sent.append(copy)
            return copy

        ring_g = [
            [
                send(x, o.at[me], (a, b), 0, "dp", right),
                send(x, o.at[me], (a, b), ahead, "dp", left),
            ]
            for x, o, a, b, _ in p_gather
        ]
        ring_r = [
            [
                send(x.at[lax.rem(me + ahead, n)], held.at[0], (a, b), 0, "dp", right),
                send(x.at[lax.rem(me + n - back, n)], held.at[ahead], (a, b), ahead, "dp", left),
            ]
            for x, o, a, b, held in p_reduce
        ]
        spread_c = []
        for x, o, a, b, _ in p_spread:
            spread_c.append(
                [
                    send(x.at[0], o.at[mine, 0], (a, b), 0, "tensor", xn),
                    send(x.at[1], o.at[mine, 1], (a, b), 1, "tensor", yn),
                    send(x.at[1], o.at[mine, 1], (a, b), 2, "tensor", xn),
                    send(x.at[0], o.at[mine, 0], (a, b), 3, "tensor", yn),
                ]
            )
        fold_c = []
        for x, o, a, b, got in p_fold:
            fold_c.append(
                [
                    send(x.at[opposite, 1], got.at[0], (a, b), 0, "tensor", xn),
                    send(x.at[opposite, 0], got.at[1], (a, b), 1, "tensor", yn),
                    send(x.at[xn, 1], got.at[2], (a, b), 2, "tensor", xn),
                    send(x.at[yn, 0], got.at[3], (a, b), 3, "tensor", yn),
                ]
            )
        for x, o, a, b, near, far in p_small:
            small_c = [
                send(x, near.at[mine], (a, b), k, "tensor", lax.rem(mine + k, t))
                for k in range(1, t)
            ]
        for x, o, a, b, local_sem in p_gather:
            kept.append(pltpu.make_async_copy(x, o.at[me], local_sem.at[0]))
            kept[-1].start()
        for x, o, a, b, local_sem in p_spread:
            kept.append(pltpu.make_async_copy(x, o.at[mine], local_sem.at[0]))
            kept[-1].start()

        def second_phase():
            for (x, o, a, b, _), c in zip(p_spread, spread_c):
                c[0].wait_recv()
                c.append(send(o.at[xn, 0], o.at[xn, 0], (a, b), 4, "tensor", yn))
                c[1].wait_recv()
                c.append(send(o.at[yn, 1], o.at[yn, 1], (a, b), 5, "tensor", xn))
            for (x, o, a, b, got), c in zip(p_fold, fold_c):
                half = x.shape[2]
                c[0].wait_recv()
                add_rows(got.at[0], [got.at[0], x.at[yn, 1]], half)
                c.append(send(got.at[0], got.at[5], (a, b), 5, "tensor", yn))
                c[1].wait_recv()
                add_rows(got.at[1], [got.at[1], x.at[xn, 0]], half)
                c.append(send(got.at[1], got.at[4], (a, b), 4, "tensor", xn))
            for x, o, a, b, near, far in p_small:
                near[mine] = x[...]
                for c in small_c:
                    c.wait_recv()
                total = near[0]
                for k in range(1, t):
                    total = total + near[k]
                far[me] = total
                for k in range(1, n):
                    small_c.append(
                        send(far.at[me], far.at[me], (a, b), t + k, "dp", lax.rem(me + k, n))
                    )

        for step in range(ahead):
            if step == middle:
                second_phase()
            for c, (x, o, a, b, _) in zip(ring_g, p_gather):
                c[0].wait_recv()
                if step < ahead - 1:
                    block = lax.rem(me - step - 1 + n, n)
                    c[0] = send(o.at[block], o.at[block], (a, b), step + 1, "dp", right)
                if step < back:
                    c[1].wait_recv()
                if step < back - 1:
                    block = lax.rem(me + step + 1, n)
                    slot = ahead + step + 1
                    c[1] = send(o.at[block], o.at[block], (a, b), slot, "dp", left)
            for c, (x, o, a, b, held) in zip(ring_r, p_reduce):
                rows = x.shape[1]
                c[0].wait_recv()
                if step < ahead - 1:
                    block = lax.rem(me + ahead - 1 - step, n)
                    add_rows(held.at[step], [held.at[step], x.at[block]], rows)
                    c[0] = send(
                        held.at[step], held.at[step + 1], (a, b), step + 1, "dp", right
                    )
                if step < back:
                    c[1].wait_recv()
                if step < back - 1:
                    block = lax.rem(me - back + 1 + step + n, n)
                    slot = ahead + step
                    add_rows(held.at[slot], [held.at[slot], x.at[block]], rows)
                    c[1] = send(
                        held.at[slot], held.at[slot + 1], (a, b), slot + 1, "dp", left
                    )
        for x, o, a, b, held in p_reduce:
            add_rows(o, [x.at[me], held.at[ahead - 1], held.at[n - 2]], x.shape[1])

        for c in spread_c:
            for k in (2, 3, 4, 5):
                c[k].wait_recv()
        for (x, o, a, b, got), c in zip(p_fold, fold_c):
            half = x.shape[2]
            for k in (2, 3, 4, 5):
                c[k].wait_recv()
            add_rows(o.at[0], [x.at[mine, 0], got.at[3], got.at[4]], half)
            add_rows(o.at[1], [x.at[mine, 1], got.at[2], got.at[5]], half)
        for x, o, a, b, near, far in p_small:
            for c in small_c[t - 1 :]:
                c.wait_recv()
            total = far[0]
            for k in range(1, n):
                total = total + far[k]
            o[...] = total
        for copy in kept:
            copy.wait()
        for copy in sent:
            copy.wait_send()

    moved = sum(array.size * array.dtype.itemsize for array in arrays)
    return pl.pallas_call(
        kernel,
        out_shape=out_shape,
        in_specs=in_specs,
        out_specs=out_specs,
        scratch_shapes=scratch,
        compiler_params=pltpu.CompilerParams(
            collective_id=identity, has_side_effects=True, vmem_limit_bytes=40 * 2**20
        ),
        cost_estimate=pl.CostEstimate(
            flops=moved, bytes_accessed=40 * moved, transcendentals=0
        ),
    )(*arrays)


def halves(rows):
    return rows.reshape(2, rows.shape[0] // 2, rows.shape[1])


def quarters(partial):
    t = lax.axis_size("tensor")
    return partial.astype(jnp.bfloat16).reshape(
        t, 2, partial.shape[0] // (2 * t), partial.shape[1]
    )


def spread_with(identity, rows, **ring):
    if lax.axis_size("tensor") == 4:
        *others, whole = exchange(identity, spread=[halves(rows)], **ring)
        return (whole.reshape(-1, rows.shape[1]), *others)
    return (gather_rows(rows), *exchange(identity, **ring))


def fold_with(identity, partial, small=None, **ring):
    if lax.axis_size("tensor") == 4:
        results = list(exchange(identity, fold=[quarters(partial)], small=small, **ring))
        total = results.pop(len(ring.get("gathers", ())) + len(ring.get("reduces", ())))
        return (total.reshape(-1, partial.shape[1]), *results)
    return (scatter_rows(partial), *exchange(identity, small=small, **ring))


def stacked(blocks):
    return blocks.reshape(-1, blocks.shape[2])


def unstacked(terms):
    n = lax.axis_size("dp")
    return terms.astype(jnp.bfloat16).reshape(n, terms.shape[0] // n, terms.shape[1])


def lagged(array, by):
    return jnp.pad(array, ((by, 0), (0, 0)))[: array.shape[0]]


def leading(array, by):
    return jnp.pad(array, ((0, by), (0, 0)))[by:]


def local(
    tokens,
    gain_one,
    in_weight,
    conv_weight,
    out_weight,
    gain_two,
    gate_weight,
    up_weight,
    down_weight,
    out_cotangent,
):
    width = tokens.shape[1]
    part = in_weight.shape[0]
    channels = in_weight.shape[2]
    units = gate_weight.shape[1]

    token_rows = tokens.astype(jnp.float32)
    normed_one, inverse_one = rms_forward(token_rows, gain_one)

    mixer_part = jnp.concatenate(
        [in_weight.reshape(part, 3 * channels), out_weight.T], axis=1
    )
    normed_all, mixer_blocks = spread_with(
        1, normed_one.astype(jnp.bfloat16), gathers=[mixer_part]
    )
    mixer_full = stacked(mixer_blocks)
    in_full = mixer_full[:, : 3 * channels]
    out_turned = mixer_full[:, 3 * channels :]
    cotangent_rows, normed_all = lax.optimization_barrier((out_cotangent, normed_all))
    cotangent_all = gather_rows(cotangent_rows)
    front_part = jnp.concatenate([gate_weight, up_weight], axis=1)

    channel_start = lax.axis_index("tensor") * channels
    taps = lax.dynamic_slice(conv_weight, (0, channel_start), (3, channels))
    row_count = normed_all.shape[0]
    positions = lax.broadcasted_iota(jnp.int32, (row_count, 1), 0) % SEQ_LEN

    projected = matmul(normed_all, in_full)
    gate_b = projected[:, :channels]
    gate_c = projected[:, channels : 2 * channels]
    values_x = projected[:, 2 * channels :]
    gated_input = gate_b * values_x
    lag_one = jnp.where(positions >= 1, lagged(gated_input, 1), 0.0)
    lag_two = jnp.where(positions >= 2, lagged(gated_input, 2), 0.0)
    convolved = taps[0] * gated_input + taps[1] * lag_one + taps[2] * lag_two
    mixer_low = (gate_c * convolved).astype(jnp.bfloat16)
    mixer_sum, front_blocks = fold_with(
        2, matmul_nt(mixer_low, out_turned), gathers=[front_part]
    )
    front_full = stacked(front_blocks)
    residual = token_rows + mixer_sum

    normed_two, inverse_two = rms_forward(residual, gain_two)
    normed_two_all, down_blocks = spread_with(
        3, normed_two.astype(jnp.bfloat16), gathers=[down_weight.T]
    )
    down_turned = stacked(down_blocks)

    front = matmul(normed_two_all, front_full)
    gate_act = front[:, :units]
    up_act = front[:, units:]
    grad_hidden = matmul(cotangent_all, down_turned)
    sigmoid_gate = jax.nn.sigmoid(gate_act)
    silu_gate = gate_act * sigmoid_gate
    hidden = (silu_gate * up_act).astype(jnp.bfloat16)
    grad_gate = (
        grad_hidden * up_act * sigmoid_gate * (1.0 + gate_act * (1.0 - sigmoid_gate))
    ).astype(jnp.bfloat16)
    grad_up = (grad_hidden * silu_gate).astype(jnp.bfloat16)
    grad_front = jnp.concatenate([grad_gate, grad_up], axis=1)
    block_out = (residual + scatter_rows(matmul_nt(hidden, down_turned))).astype(jnp.bfloat16)

    down_terms = matmul_tn(cotangent_all, hidden)
    grad_two, down_grad = fold_with(
        4, matmul_nt(grad_front, front_full), reduces=[unstacked(down_terms)]
    )
    front_terms = matmul_tn(normed_two_all, grad_front)
    gain_two_grad = (
        jnp.sum(front_terms * front_full.astype(jnp.float32), axis=1) / gain_two
    )

    grad_resid = out_cotangent.astype(jnp.float32) + rms_backward(
        residual, inverse_two, gain_two, grad_two
    )
    branch_all, front_grad = spread_with(
        5, grad_resid.astype(jnp.bfloat16), reduces=[unstacked(front_terms)]
    )

    grad_mixer = matmul(branch_all, out_turned)
    out_terms = matmul_tn(branch_all, mixer_low)
    grad_conv = grad_mixer * gate_c
    lead_one = leading(jnp.where(positions >= 1, grad_conv, 0.0), 1)
    lead_two = leading(jnp.where(positions >= 2, grad_conv, 0.0), 2)
    grad_gated = taps[0] * grad_conv + taps[1] * lead_one + taps[2] * lead_two
    grad_proj = jnp.concatenate(
        [
            (grad_gated * values_x).astype(jnp.bfloat16),
            (grad_mixer * convolved).astype(jnp.bfloat16),
            (grad_gated * gate_b).astype(jnp.bfloat16),
        ],
        axis=1,
    )
    in_terms = matmul_tn(normed_all, grad_proj)
    tap_grad = jnp.stack(
        [
            jnp.sum(grad_conv * gated_input, axis=0),
            jnp.sum(grad_conv * lag_one, axis=0),
            jnp.sum(grad_conv * lag_two, axis=0),
        ]
    )
    gain_one_grad = jnp.sum(in_terms * in_full.astype(jnp.float32), axis=1) / gain_one
    tap_full = lax.dynamic_update_slice(
        jnp.zeros((3, width), jnp.float32), tap_grad, (0, channel_start)
    )
    small = jnp.concatenate(
        [gain_one_grad[None], gain_two_grad[None], tap_full, jnp.zeros_like(tap_full)], axis=0
    )
    mixer_terms = jnp.concatenate(
        [in_terms.astype(jnp.bfloat16), out_terms.astype(jnp.bfloat16)], axis=1
    )
    grad_one, mixer_grad, small = fold_with(
        6, matmul_nt(grad_proj, in_full), small=small, reduces=[unstacked(mixer_terms)]
    )

    token_grad = grad_resid + rms_backward(token_rows, inverse_one, gain_one, grad_one)
    return (
        block_out,
        token_grad,
        small[0],
        mixer_grad[:, : 3 * channels].reshape(part, 3, channels),
        small[2:5],
        mixer_grad[:, 3 * channels :].T,
        small[1],
        front_grad[:, :units],
        front_grad[:, units:],
        down_grad.T,
    )


def solution(mesh):
    return jax.shard_map(
        local,
        mesh=mesh,
        in_specs=(
            P(("dp", "tensor"), None),
            P(),
            P("dp", None, "tensor"),
            P(),
            P("tensor", "dp"),
            P(),
            P("dp", "tensor"),
            P("dp", "tensor"),
            P("tensor", "dp"),
            P(("dp", "tensor"), None),
        ),
        out_specs=(
            P(("dp", "tensor"), None),
            P(("dp", "tensor"), None),
            P(),
            P("dp", None, "tensor"),
            P(),
            P("tensor", "dp"),
            P(),
            P("dp", "tensor"),
            P("dp", "tensor"),
            P("tensor", "dp"),
        ),
        check_vma=False,
    )
```
